32 devices in a mesh: tm: 8 (over z, core), space: 4 (over y, x).
Axes of the slice: x: 2, y: 2, z: 4, core: 2. Of those that a mesh axis runs over, the one named last changes fastest.
Arguments:
- starts: float32 [8, 48, 64, 128], P('tm', 'space'), may hold values from -45 to 45
- vel_x: float32 [48, 64, 128], P('space'), may hold values from -0.15 to 0.15
- vel_y: float32 [48, 64, 128], P('space'), may hold values from -0.15 to 0.15
- vel_z: float32 [48, 64, 128], P('space'), may hold values from -0.5 to 0.5
- kappa: float32 [48, 64, 128], P('space'), may hold values from 0.01 to 0.03
Outputs:
- new_starts: float32 [8, 48, 64, 128], P('tm', 'space')
- change_norm: float32 [], replicated
The draws below stay inside these ranges and needn't reach their ends.
All inputs are finite; a program needn't handle non-finite values.
Results may differ from the reference program's by a relative error of at most 0.0003.
Values sent between devices are 32-bit elements; how exact they have to be, the bound alone decides.
A program may use at most 128 MiB of HBM per device.

```python
import math
import jax
import jax.numpy as jnp
from jax import lax

NX = 128
NY = 64
FSTEPS = 6
GC = 2
NZ = 48
SLICES = 8


def draw_starts(key, part):
    key_base = jax.random.fold_in(key, 11)
    key_rows = jax.random.fold_in(key, 12)
    key_cols = jax.random.fold_in(key, 13)
    shape = (SLICES, NZ, NY, NX)
    slice_pos = jnp.arange(SLICES, dtype=jnp.float32) / max(SLICES - 1, 1)
    depth_pos = jnp.arange(NZ, dtype=jnp.float32) / max(NZ - 1, 1)
    amplitude = jnp.sqrt((1.0 + 3.0 * slice_pos)[:, None, None, None] * (1.0 + 2.0 * depth_pos)[None, :, None, None])
    row_scale = jnp.exp(jax.random.uniform(key_rows, (NY,), jnp.float32, math.log(0.5), math.log(1.6)))
    col_scale = jnp.exp(jax.random.uniform(key_cols, (NX,), jnp.float32, math.log(0.5), math.log(1.6)))
    base = jax.random.truncated_normal(key_base, -5.0, 5.0, shape, jnp.float32)
    values = base * amplitude * row_scale[None, None, :, None] * col_scale[None, None, None, :]
    return values.astype(jnp.float32)


def steps_of(rng, extent, shards, low, largest):
    def one(dim, blocks):
        draws = jax.random.uniform(jax.random.fold_in(jax.random.fold_in(rng, 6), dim), (blocks,), jnp.float32, low / len(shards), largest / len(shards))
        return jnp.repeat(jnp.exp(draws), extent[dim] // blocks).reshape((-1,) + (1,) * (len(extent) - dim - 1))

    level = one(*shards[0])
    for cut in shards[1:]:
        level = level * one(*cut)
    return level


def setup_inputs(seed: int = 0) -> dict:
    splits = jax.random.split(jax.random.key(seed), 6)
    starts = draw_starts(jax.random.fold_in(splits[5], 71), 0)
    vel_x = jnp.clip(jax.random.uniform(splits[1], (NZ, NY, NX), jnp.float32, -0.15, 0.15) * steps_of(splits[1], (NZ, NY, NX), ((0, 4),), -0.4, 0.0), -0.15, 0.15)
    vel_y = jnp.clip(jax.random.uniform(splits[2], (NZ, NY, NX), jnp.float32, -0.15, 0.15) * steps_of(splits[2], (NZ, NY, NX), ((0, 4),), -0.4, 0.0), -0.15, 0.15)
    vel_z = jnp.clip(jax.random.uniform(splits[3], (NZ, NY, NX), jnp.float32, -0.5, 0.5) * steps_of(splits[3], (NZ, NY, NX), ((0, 4),), -0.4, 0.0), -0.5, 0.5)
    kappa = jnp.clip(jnp.exp(math.log(0.03) - 1.0986123 * jax.random.uniform(splits[4], (NZ, NY, NX), jnp.float32) ** steps_of(splits[4], (NZ, NY, NX), ((0, 4),), -0.2, 0.2)), 0.01, 0.03)
    return dict(starts=starts, vel_x=vel_x, vel_y=vel_y, vel_z=vel_z, kappa=kappa)


def advance(extended, vel_x, vel_y, vel_z, kappa):
    padded = jnp.pad(extended, ((0, 0), (1, 1), (1, 1)))
    center = padded[1:-1, 1:-1, 1:-1]
    z_minus = padded[:-2, 1:-1, 1:-1]
    z_plus = padded[2:, 1:-1, 1:-1]
    y_minus = padded[1:-1, :-2, 1:-1]
    y_plus = padded[1:-1, 2:, 1:-1]
    x_minus = padded[1:-1, 1:-1, :-2]
    x_plus = padded[1:-1, 1:-1, 2:]
    transport = jnp.maximum(vel_x, 0.0) * (center - x_minus) + jnp.minimum(vel_x, 0.0) * (x_plus - center)
    transport = transport + (jnp.maximum(vel_y, 0.0) * (center - y_minus) + jnp.minimum(vel_y, 0.0) * (y_plus - center))
    transport = transport + (jnp.maximum(vel_z, 0.0) * (center - z_minus) + jnp.minimum(vel_z, 0.0) * (z_plus - center))
    diffusion = kappa * (x_minus + x_plus + y_minus + y_plus + z_minus + z_plus - 6.0 * center)
    return center - transport + diffusion

def zpad(field):
    return jnp.pad(field, ((1, 1), (0, 0), (0, 0)))

def restrict(field):
    depth, rows, cols = field.shape
    return field.reshape(depth // 4, 4, rows // 4, 4, cols // 4, 4).mean(axis=(1, 3, 5))

def prolong(field):
    depth, rows, cols = field.shape
    wide = jnp.broadcast_to(field[:, None, :, None, :, None], (depth, 4, rows, 4, cols, 4))
    return wide.reshape(depth * 4, rows * 4, cols * 4)

def reference(starts, vel_x, vel_y, vel_z, kappa):
    courant_scale = FSTEPS / (4.0 * GC)
    diffusion_scale = FSTEPS / (16.0 * GC)
    coarse_x = restrict(vel_x) * courant_scale
    coarse_y = restrict(vel_y) * courant_scale
    coarse_z = restrict(vel_z) * courant_scale
    coarse_k = restrict(kappa) * diffusion_scale

    def fine(field):
        for step_index in range(FSTEPS):
            field = advance(zpad(field), vel_x, vel_y, vel_z, kappa)
        return field

    def coarse(field):
        for step_index in range(GC):
            field = advance(zpad(field), coarse_x, coarse_y, coarse_z, coarse_k)
        return field
    fine_ends = lax.map(fine, starts)
    coarse_now = restrict(starts[0])
    new_list = [starts[0]]
    for slice_index in range(SLICES - 1):
        fine_coarse = restrict(fine_ends[slice_index])
        drift_term = fine_coarse - coarse(restrict(starts[slice_index]))
        coarse_now = coarse(coarse_now) + drift_term
        new_list.append(fine_ends[slice_index] + prolong(coarse_now - fine_coarse))
    new_starts = jnp.stack(new_list)
    total_sum = jnp.sum((new_starts - starts) ** 2)
    change_norm = jnp.sqrt(total_sum / (SLICES * NZ * NY * NX) + 1e-06)
    return (new_starts, change_norm)
```

```python
import functools

import jax
import jax.numpy as jnp
from jax import lax
from jax.experimental import pallas as pl
from jax.experimental.pallas import tpu as pltpu
from jax.sharding import PartitionSpec as P

FSTEPS = 6
GC = 2
B = 4
ROUNDS = (2, 2, 2)
HALO = max(ROUNDS)
MESH = pl.DeviceIdType.MESH


def dot(a, b):
    return jnp.dot(
        a, b, precision=lax.Precision.HIGHEST, preferred_element_type=jnp.float32
    )


def iota(shape, dim):
    return lax.broadcasted_iota(jnp.int32, shape, dim)


def group_mask(rows, lanes):
    group = (iota((rows, lanes), 0) // B) % B
    return group == iota((rows, lanes), 1) // (lanes // B)


def pool(sums, packed_rows):
    rows, lanes = sums.shape
    cols = lanes // B
    spread = iota((lanes, lanes), 0) // B == iota((lanes, lanes), 1) % cols
    wide = dot(sums, jnp.where(spread, 1.0 / B**3, 0.0).astype(jnp.float32))
    wide = jnp.where(group_mask(rows, lanes), wide, 0.0)
    pick = iota((packed_rows, rows), 1) // B**2 == iota((packed_rows, rows), 0)
    return dot(pick.astype(jnp.float32), wide)


def prolong(packed, rows, first):
    lanes = packed.shape[1]
    cols = lanes // B
    shape = (rows, packed.shape[0])
    pick = iota(shape, 0) // B**2 + first == iota(shape, 1)
    wide = dot(pick.astype(jnp.float32), packed)
    wide = jnp.where(group_mask(rows, lanes), wide, 0.0)
    spread = iota((lanes, lanes), 0) % cols == iota((lanes, lanes), 1) // B
    return dot(wide, spread.astype(jnp.float32))


def weights(vx, vy, vz, k, edges):
    low_x, high_x, low_y, high_y, low_z, high_z = edges

    def inside(edge, value):
        return value if edge is None else jnp.where(edge, 0.0, value)

    return (
        1.0 - jnp.abs(vx) - jnp.abs(vy) - jnp.abs(vz) - 6.0 * k,
        inside(low_x, k + jnp.maximum(vx, 0.0)),
        inside(high_x, k - jnp.minimum(vx, 0.0)),
        inside(low_y, k + jnp.maximum(vy, 0.0)),
        inside(high_y, k - jnp.minimum(vy, 0.0)),
        inside(low_z, k + jnp.maximum(vz, 0.0)),
        inside(high_z, k - jnp.minimum(vz, 0.0)),
    )


def kernel(
    T, S,
    st_hbm, vx_hbm, vy_hbm, vz_hbm, kp_hbm,
    out_ref, chg_ref,
    cx, co, U, V, st, F, wloc, wg, ccloc, ccg, qloc, qg, full, cfull, cw, hs,
    lsem, usend, urecv, csend, crecv, hsend, hrecv, ccsend, ccrecv,
    wsend, wrecv, qsend, qrecv,
):
    depth, Y, X = st.shape
    N = T * S
    t = lax.axis_index("tm")
    s = lax.axis_index("space")
    me = t * S + s
    planes = depth // B
    slab_rows = planes * Y // B**2
    plane_rows = Y // B**2
    pad_rows = wloc.shape[0]
    H = HALO
    coefs = (vx_hbm, vy_hbm, vz_hbm, kp_hbm)

    def peer(i):
        return lax.rem(t + i // S, T), lax.rem(s + lax.rem(i, S), S)

    loads = [
        pltpu.make_async_copy(c, cx.at[i, pl.ds(H - 1, depth)], lsem.at[i])
        for i, c in enumerate(coefs)
    ]
    load_st = pltpu.make_async_copy(st_hbm.at[0], st, lsem.at[4])
    for c in loads:
        c.start()
    load_st.start()

    barrier = pltpu.get_barrier_semaphore()

    def greet(i, _):
        pl.semaphore_signal(barrier, inc=1, device_id=peer(i), device_id_type=MESH)
        return 0

    lax.fori_loop(1, N, greet, 0)

    @pl.when(s == 0)
    def _():
        for r in range(len(ROUNDS)):
            U[r, 0:H] = jnp.zeros((H, Y, X), jnp.float32)
        if H > 1:
            cx[:, 0 : H - 1] = jnp.zeros((4, H - 1, Y, X), jnp.float32)

    @pl.when(s == S - 1)
    def _():
        for r in range(len(ROUNDS)):
            U[r, H + depth : 2 * H + depth] = jnp.zeros((H, Y, X), jnp.float32)
        if H > 1:
            cx[:, H - 1 + depth : 2 * H - 2 + depth] = jnp.zeros((4, H - 1, Y, X), jnp.float32)

    for c in loads:
        c.wait()
    load_st.wait()

    lane = iota((Y, X), 1)
    row = iota((Y, X), 0)
    edges = (lane == 0, lane == X - 1, row == 0, row == Y - 1, None, None)

    def fill(z, _):
        for i, w in enumerate(weights(cx[0, z], cx[1, z], cx[2, z], cx[3, z], edges)):
            co[i, z] = w
        return 0

    lax.fori_loop(H - 1, H - 1 + depth, fill, 0)

    for i in range(4):
        sums = [
            cx[i, H - 1 + B * p] + cx[i, H + B * p] + cx[i, H + 1 + B * p] + cx[i, H + 2 + B * p]
            for p in range(planes)
        ]
        ccloc[i] = pool(jnp.concatenate(sums, axis=0), pad_rows)
    ccg[pl.ds(s, 1)] = ccloc[...][None]

    pl.semaphore_wait(barrier, N - 1)

    def remote(src, dst, send, recv, device):
        return pltpu.make_async_remote_copy(
            src_ref=src, dst_ref=dst, send_sem=send, recv_sem=recv,
            device_id=device, device_id_type=MESH,
        )

    d0 = ROUNDS[0]
    up_t = lax.rem(t + 1, T)
    up_s = lax.rem(s + 1, S)
    down_s = lax.rem(s + S - 1, S)
    has_up = s < S - 1
    has_down = s > 0
    moves = t < T - 1
    works = t > 0
    low0 = remote(st_hbm.at[0, pl.ds(depth - d0, d0)], U.at[0, pl.ds(H - d0, d0)],
                  usend.at[0], urecv.at[0], (up_t, up_s))
    high0 = remote(st_hbm.at[0, pl.ds(0, d0)], U.at[0, pl.ds(H + depth, d0)],
                   usend.at[1], urecv.at[1], (up_t, down_s))
    main0 = remote(st_hbm.at[0], U.at[0, pl.ds(H, depth)],
                   usend.at[2], urecv.at[2], (up_t, s))
    low_c = [
        remote(c.at[pl.ds(depth - H + 1, H - 1)], cx.at[i, pl.ds(0, H - 1)],
               csend.at[0, i], crecv.at[0, i], (t, up_s))
        for i, c in enumerate(coefs)
    ] if H > 1 else []
    high_c = [
        remote(c.at[pl.ds(0, H - 1)], cx.at[i, pl.ds(H - 1 + depth, H - 1)],
               csend.at[1, i], crecv.at[1, i], (t, down_s))
        for i, c in enumerate(coefs)
    ] if H > 1 else []

    @pl.when(moves)
    def _():
        main0.start()

    @pl.when(moves & has_up)
    def _():
        low0.start()

    @pl.when(moves & has_down)
    def _():
        high0.start()

    @pl.when(works & has_up)
    def _():
        for c in low_c:
            c.start()

    @pl.when(works & has_down)
    def _():
        for c in high_c:
            c.start()

    def cc_copy(j, slot):
        return remote(ccloc, ccg.at[slot], ccsend.at[j], ccrecv.at[slot],
                      (t, lax.rem(s + j, S)))

    for j in range(1, S):
        cc_copy(j, s).start()

    def step(src, dst, lo, hi):
        def body(z, _):
            u = src[z]
            v = co[0, z - 1] * u
            v += co[1, z - 1] * pltpu.roll(u, 1, 1)
            v += co[2, z - 1] * pltpu.roll(u, X - 1, 1)
            v += co[3, z - 1] * pltpu.roll(u, 1, 0)
            v += co[4, z - 1] * pltpu.roll(u, Y - 1, 0)
            v += co[5, z - 1] * src[z - 1]
            v += co[6, z - 1] * src[z + 1]
            dst[z] = v
            return 0

        lax.fori_loop(lo, hi, body, 0)

    def w_copy(i, slot):
        return remote(wloc.at[pl.ds(0, slab_rows)], wg.at[slot, pl.ds(0, slab_rows)],
                      wsend.at[i], wrecv.at[slot], peer(i))

    def q_copy(i, slot):
        return remote(qloc, qg.at[slot], qsend.at[i], qrecv.at[slot], peer(i))

    @pl.when(works)
    def _():
        @pl.when(has_down)
        def _():
            for c in low_c:
                c.wait_recv()
            lax.fori_loop(0, H - 1, fill, 0)
            low0.wait_recv()

        @pl.when(has_up)
        def _():
            for c in high_c:
                c.wait_recv()
            lax.fori_loop(H - 1 + depth, 2 * H - 2 + depth, fill, 0)
            high0.wait_recv()

        @pl.when(s == 0)
        def _():
            lax.fori_loop(0, H - 1, fill, 0)

        @pl.when(s == S - 1)
        def _():
            lax.fori_loop(H - 1 + depth, 2 * H - 2 + depth, fill, 0)

        main0.wait_recv()

        for r, d in enumerate(ROUNDS):
            if r > 0:
                low = remote(U.at[r, pl.ds(H + depth - d, d)], U.at[r, pl.ds(H - d, d)],
                             hsend.at[r, 0], hrecv.at[r, 0], (t, up_s))
                high = remote(U.at[r, pl.ds(H, d)], U.at[r, pl.ds(H + depth, d)],
                              hsend.at[r, 1], hrecv.at[r, 1], (t, down_s))

                @pl.when(has_up)
                def _(low=low):
                    low.start()

                @pl.when(has_down)
                def _(high=high):
                    high.start()

                @pl.when(has_down)
                def _(low=low):
                    low.wait_recv()

                @pl.when(has_up)
                def _(high=high):
                    high.wait_recv()
            src = U.at[r]
            for j in range(1, d + 1):
                dst = U.at[r + 1] if j == d else V.at[j % 2]
                step(src, dst, H - d + j, H + depth + d - j)
                src = dst
            if r > 0:
                @pl.when(has_up)
                def _(low=low):
                    low.wait_send()

                @pl.when(has_down)
                def _(high=high):
                    high.wait_send()

        R = len(ROUNDS)
        sums = []
        for p in range(planes):
            total = None
            for z in range(B * p, B * p + B):
                f = U[R, H + z] - st[z]
                F[z] = f
                total = f if total is None else total + f
            sums.append(total)
        wloc[...] = pool(jnp.concatenate(sums, axis=0), pad_rows)

        def send_w(i, _):
            w_copy(i, me).start()
            return 0

        lax.fori_loop(1, N, send_w, 0)
        wg[pl.ds(me, 1)] = wloc[...][None]

        wide = prolong(wloc[...], planes * Y, 0)
        q = jnp.zeros((8, X), jnp.float32)
        for p in range(planes):
            mean = wide[p * Y : (p + 1) * Y]
            for z in range(B * p, B * p + B):
                g = F[z] - mean
                q += jnp.sum((g * g).reshape(Y // 8, 8, X), axis=0)
        qloc[...] = jnp.sum(q, axis=0, keepdims=True)

        def send_q(i, _):
            q_copy(i, me).start()
            return 0

        lax.fori_loop(1, N, send_q, 0)
        qg[pl.ds(me, 1)] = qloc[...][None]

    for j in range(1, S):
        cc_copy(j, lax.rem(s + S - j, S)).wait_recv()
    for p in range(S):
        cfull[:, p * slab_rows : (p + 1) * slab_rows] = ccg[p, :, 0:slab_rows]
    rows = S * slab_rows
    crow = iota((rows, X), 0)
    clane = iota((rows, X), 1)
    cols = X // B
    group = clane // cols
    y_high = lax.rem(crow, plane_rows)
    courant = FSTEPS / (4.0 * GC)
    spread = FSTEPS / (16.0 * GC)
    for i, w in enumerate(weights(
        cfull[0] * courant, cfull[1] * courant, cfull[2] * courant, cfull[3] * spread,
        (
            lax.rem(clane, cols) == 0,
            lax.rem(clane, cols) == cols - 1,
            (y_high == 0) & (group == 0),
            (y_high == plane_rows - 1) & (group == B - 1),
            crow < plane_rows,
            crow >= rows - plane_rows,
        ),
    )):
        cw[i] = w

    def coarse(u):
        for _ in range(GC):
            below = jnp.where(group == B - 1, pltpu.roll(u, 1, 0), u)
            above = jnp.where(group == 0, pltpu.roll(u, rows - 1, 0), u)
            v = cw[0] * u
            v += cw[1] * pltpu.roll(u, 1, 1)
            v += cw[2] * pltpu.roll(u, X - 1, 1)
            v += cw[3] * pltpu.roll(below, cols, 1)
            v += cw[4] * pltpu.roll(above, X - cols, 1)
            v += cw[5] * pltpu.roll(u, plane_rows, 0)
            v += cw[6] * pltpu.roll(u, rows - plane_rows, 0)
            u = v
        return u

    def arrival(copy, slot):
        @pl.when(slot != me)
        def _():
            copy(1, slot).wait_recv()

    def chain(m, carry):
        jump, squares = carry
        for p in range(S):
            arrival(w_copy, m * S + p)
        for p in range(S):
            full[p * slab_rows : (p + 1) * slab_rows] = wg[m * S + p, 0:slab_rows]
        moved = coarse(jump)
        hs[m] = moved
        jump = full[...] + moved
        return jump, squares + jump * jump

    zero = jnp.zeros((rows, X), jnp.float32)
    _, squares = lax.fori_loop(1, T, chain, (zero, zero))

    @pl.when(works)
    def _():
        wide = prolong(hs[t], planes * Y, s * slab_rows)
        for z in range(depth):
            p = z // B
            out_ref[0, z] = U[len(ROUNDS), H + z] + wide[p * Y : (p + 1) * Y]

    @pl.when(t == 0)
    def _():
        out_ref[0] = st[...]

    def gather_q(i, total):
        arrival(q_copy, i)
        return total + qg[i]

    total = lax.fori_loop(S, N, gather_q, jnp.zeros((1, X), jnp.float32))
    total = total + float(B**3) * jnp.sum(squares, axis=0, keepdims=True)
    total = jnp.sum(total, axis=1, keepdims=True)
    count = N * depth * Y * X
    chg_ref[...] = jnp.sqrt(total / count + 1e-6)

    for j in range(1, S):
        cc_copy(j, s).wait_send()

    @pl.when(moves)
    def _():
        main0.wait_send()

    @pl.when(moves & has_up)
    def _():
        low0.wait_send()

    @pl.when(moves & has_down)
    def _():
        high0.wait_send()

    @pl.when(works & has_up)
    def _():
        for c in low_c:
            c.wait_send()

    @pl.when(works & has_down)
    def _():
        for c in high_c:
            c.wait_send()

    @pl.when(works)
    def _():
        def done(i, _):
            w_copy(i, me).wait_send()
            q_copy(i, me).wait_send()
            return 0

        lax.fori_loop(1, N, done, 0)


def per_device(T, S, starts, vel_x, vel_y, vel_z, kappa):
    depth, Y, X = vel_x.shape
    slab_rows = depth // B * Y // B**2
    pad_rows = -(-slab_rows // 8) * 8
    rows = S * slab_rows
    N = T * S
    R = len(ROUNDS)
    vmem = lambda *shape: pltpu.VMEM(shape, jnp.float32)
    dma = lambda *shape: pltpu.SemaphoreType.DMA(shape)
    ext = depth + 2 * HALO
    new, change = pl.pallas_call(
        functools.partial(kernel, T, S),
        out_shape=(
            jax.ShapeDtypeStruct(starts.shape, jnp.float32),
            jax.ShapeDtypeStruct((1, 1), jnp.float32),
        ),
        in_specs=[pl.BlockSpec(memory_space=pl.ANY)] * 5,
        out_specs=(
            pl.BlockSpec(memory_space=pltpu.VMEM),
            pl.BlockSpec(memory_space=pltpu.VMEM),
        ),
        scratch_shapes=[
            vmem(4, ext - 2, Y, X),
            vmem(7, ext - 2, Y, X),
            vmem(R + 1, ext, Y, X),
            vmem(2, ext, Y, X),
            vmem(depth, Y, X),
            vmem(depth, Y, X),
            vmem(pad_rows, X),
            vmem(N, pad_rows, X),
            vmem(4, pad_rows, X),
            vmem(S, 4, pad_rows, X),
            vmem(1, X),
            vmem(N, 1, X),
            vmem(rows, X),
            vmem(4, rows, X),
            vmem(7, rows, X),
            vmem(T, rows, X),
            dma(5),
            dma(3), dma(3),
            dma(2, 4), dma(2, 4),
            dma(R, 2), dma(R, 2),
            dma(S), dma(S),
            dma(N), dma(N),
            dma(N), dma(N),
        ],
        compiler_params=pltpu.CompilerParams(
            collective_id=0, has_side_effects=True, vmem_limit_bytes=40 * 2**20
        ),
    )(starts, vel_x, vel_y, vel_z, kappa)
    return new, change[0, 0]


def solution(mesh):
    T, S = mesh.shape["tm"], mesh.shape["space"]
    return jax.shard_map(
        functools.partial(per_device, T, S),
        mesh=mesh,
        in_specs=(
            P("tm", "space", None, None),
            P("space", None, None),
            P("space", None, None),
            P("space", None, None),
            P("space", None, None),
        ),
        out_specs=(P("tm", "space", None, None), P()),
        check_vma=False,
    )
```

```python
import functools

import jax
import jax.numpy as jnp
from jax import lax
from jax.experimental import pallas as pl
from jax.experimental.pallas import tpu as pltpu
from jax.sharding import PartitionSpec as P

FSTEPS = 6
GC = 2
B = 4
ROUNDS = (2, 2, 2)
HALO = max(ROUNDS)
STEP_PLANES = (14, 12, 7, 4, 2, 1)
MESH = pl.DeviceIdType.MESH


def dot(a, b):
    return jnp.dot(
        a, b, precision=lax.Precision.HIGHEST, preferred_element_type=jnp.float32
    )


def iota(shape, dim):
    return lax.broadcasted_iota(jnp.int32, shape, dim)


def group_mask(rows, lanes):
    group = (iota((rows, lanes), 0) // B) % B
    return group == iota((rows, lanes), 1) // (lanes // B)


def pool(sums, packed_rows):
    rows, lanes = sums.shape
    cols = lanes // B
    spread = iota((lanes, lanes), 0) // B == iota((lanes, lanes), 1) % cols
    wide = dot(sums, jnp.where(spread, 1.0 / B**3, 0.0).astype(jnp.float32))
    wide = jnp.where(group_mask(rows, lanes), wide, 0.0)
    pick = iota((packed_rows, rows), 1) // B**2 == iota((packed_rows, rows), 0)
    return dot(pick.astype(jnp.float32), wide)


def prolong(packed, rows, first):
    lanes = packed.shape[1]
    cols = lanes // B
    shape = (rows, packed.shape[0])
    pick = iota(shape, 0) // B**2 + first == iota(shape, 1)
    wide = dot(pick.astype(jnp.float32), packed)
    wide = jnp.where(group_mask(rows, lanes), wide, 0.0)
    spread = iota((lanes, lanes), 0) % cols == iota((lanes, lanes), 1) // B
    return dot(wide, spread.astype(jnp.float32))


def weights(vx, vy, vz, k, edges):
    low_x, high_x, low_y, high_y, low_z, high_z = edges

    def inside(edge, value):
        return value if edge is None else jnp.where(edge, 0.0, value)

    return (
        1.0 - jnp.abs(vx) - jnp.abs(vy) - jnp.abs(vz) - 6.0 * k,
        inside(low_x, k + jnp.maximum(vx, 0.0)),
        inside(high_x, k - jnp.minimum(vx, 0.0)),
        inside(low_y, k + jnp.maximum(vy, 0.0)),
        inside(high_y, k - jnp.minimum(vy, 0.0)),
        inside(low_z, k + jnp.maximum(vz, 0.0)),
        inside(high_z, k - jnp.minimum(vz, 0.0)),
    )


def kernel(
    T, S,
    st_hbm, vx_hbm, vy_hbm, vz_hbm, kp_hbm,
    out_ref, chg_ref,
    cx, co, U, V, st, F, wloc, wg, ccloc, ccg, qloc, qg, qsum, qsums, full, cfull, cw, hs,
    lsem, usend, urecv, csend, crecv, hsend, hrecv, ccsend, ccrecv,
    wsend, wrecv, qsend, qrecv, ysend, yrecv, ready,
):
    depth, Y, X = st.shape
    N = T * S
    t = lax.axis_index("tm")
    s = lax.axis_index("space")
    planes = depth // B
    slab_rows = planes * Y // B**2
    plane_rows = Y // B**2
    pad_rows = wloc.shape[0]
    H = HALO
    coefs = (vx_hbm, vy_hbm, vz_hbm, kp_hbm)

    loads = [
        pltpu.make_async_copy(c, cx.at[i, pl.ds(H - 1, depth)], lsem.at[i])
        for i, c in enumerate(coefs)
    ]
    load_st = pltpu.make_async_copy(st_hbm.at[0], st, lsem.at[4])
    for c in loads:
        c.start()
    load_st.start()

    barrier = pltpu.get_barrier_semaphore()

    up_t = lax.rem(t + 1, T)
    down_t = lax.rem(t + T - 1, T)
    up_s = lax.rem(s + 1, S)
    down_s = lax.rem(s + S - 1, S)
    has_up = s < S - 1
    has_down = s > 0
    moves = t < T - 1
    works = t > 0

    def greet(device):
        pl.semaphore_signal(barrier, inc=1, device_id=device, device_id_type=MESH)

    @pl.when(works & has_up)
    def _():
        greet((down_t, up_s))

    @pl.when(works & has_down)
    def _():
        greet((down_t, down_s))

    for j in range(1, T):
        greet((lax.rem(t + j, T), s))
    for j in range(1, S):
        greet((t, lax.rem(s + j, S)))

    @pl.when(s == 0)
    def _():
        for r in range(len(ROUNDS)):
            U[r, 0:H] = jnp.zeros((H, Y, X), jnp.float32)
        if H > 1:
            cx[:, 0 : H - 1] = jnp.zeros((4, H - 1, Y, X), jnp.float32)

    @pl.when(s == S - 1)
    def _():
        for r in range(len(ROUNDS)):
            U[r, H + depth : 2 * H + depth] = jnp.zeros((H, Y, X), jnp.float32)
        if H > 1:
            cx[:, H - 1 + depth : 2 * H - 2 + depth] = jnp.zeros((4, H - 1, Y, X), jnp.float32)

    for c in loads:
        c.wait()
    load_st.wait()

    lane = iota((Y, X), 1)
    row = iota((Y, X), 0)
    edges = (lane == 0, lane == X - 1, row == 0, row == Y - 1, None, None)

    def fill(z, _):
        for i, w in enumerate(weights(cx[0, z], cx[1, z], cx[2, z], cx[3, z], edges)):
            co[i, z] = w
        return 0

    lax.fori_loop(H - 1, H - 1 + depth, fill, 0)

    for i in range(4):
        sums = [
            cx[i, H - 1 + B * p] + cx[i, H + B * p] + cx[i, H + 1 + B * p] + cx[i, H + 2 + B * p]
            for p in range(planes)
        ]
        ccloc[i] = pool(jnp.concatenate(sums, axis=0), pad_rows)
    ccg[pl.ds(s, 1)] = ccloc[...][None]

    across = jnp.where(has_up, 1, 0) + jnp.where(has_down, 1, 0)
    pl.semaphore_wait(barrier, T + S - 2 + jnp.where(moves, across, 0))

    for j in range(1, S):
        pl.semaphore_signal(
            ready, inc=1, device_id=(t, lax.rem(s + j, S)), device_id_type=MESH
        )

    def remote(src, dst, send, recv, device):
        return pltpu.make_async_remote_copy(
            src_ref=src, dst_ref=dst, send_sem=send, recv_sem=recv,
            device_id=device, device_id_type=MESH,
        )

    d0 = ROUNDS[0]
    low0 = remote(st_hbm.at[0, pl.ds(depth - d0, d0)], U.at[0, pl.ds(H - d0, d0)],
                  usend.at[0], urecv.at[0], (up_t, up_s))
    high0 = remote(st_hbm.at[0, pl.ds(0, d0)], U.at[0, pl.ds(H + depth, d0)],
                   usend.at[1], urecv.at[1], (up_t, down_s))
    main0 = remote(st_hbm.at[0], U.at[0, pl.ds(H, depth)],
                   usend.at[2], urecv.at[2], (up_t, s))
    low_c = [
        remote(c.at[pl.ds(depth - H + 1, H - 1)], cx.at[i, pl.ds(0, H - 1)],
               csend.at[0, i], crecv.at[0, i], (t, up_s))
        for i, c in enumerate(coefs)
    ] if H > 1 else []
    high_c = [
        remote(c.at[pl.ds(0, H - 1)], cx.at[i, pl.ds(H - 1 + depth, H - 1)],
               csend.at[1, i], crecv.at[1, i], (t, down_s))
        for i, c in enumerate(coefs)
    ] if H > 1 else []

    @pl.when(moves)
    def _():
        main0.start()

    @pl.when(moves & has_up)
    def _():
        low0.start()

    @pl.when(moves & has_down)
    def _():
        high0.start()

    @pl.when(works & has_up)
    def _():
        for c in low_c:
            c.start()

    @pl.when(works & has_down)
    def _():
        for c in high_c:
            c.start()

    def cc_copy(j, slot):
        return remote(ccloc, ccg.at[slot], ccsend.at[j], ccrecv.at[slot],
                      (t, lax.rem(s + j, S)))

    for j in range(1, S):
        cc_copy(j, s).start()

    def step(src, dst, lo, hi):
        group = next(g for g in STEP_PLANES if (hi - lo) % g == 0)

        def body(i, _):
            z = lo + i * group
            u = [src[z - 1 + k] for k in range(group + 2)]
            new = []
            for k in range(group):
                c, n = u[k + 1], z - 1 + k
                v = co[0, n] * c + co[5, n] * u[k] + co[6, n] * u[k + 2]
                v += co[3, n] * pltpu.roll(c, 1, 0) + co[4, n] * pltpu.roll(c, Y - 1, 0)
                v += co[1, n] * pltpu.roll(c, 1, 1) + co[2, n] * pltpu.roll(c, X - 1, 1)
                new.append(v)
            for k in range(group):
                dst[z + k] = new[k]
            return 0

        lax.fori_loop(0, (hi - lo) // group, body, 0)

    def w_copy(j, k, slice_from, place):
        return remote(wloc.at[pl.ds(0, slab_rows)],
                      wg.at[place, slice_from, pl.ds(0, slab_rows)],
                      wsend.at[j, k], wrecv.at[place, slice_from],
                      (lax.rem(t + j, T), lax.rem(s + k, S)))

    def q_copy(j, slice_from):
        return remote(qloc, qg.at[slice_from], qsend.at[j], qrecv.at[slice_from],
                      (lax.rem(t + j, T), s))

    def sum_copy(j, place):
        return remote(qsum, qsums.at[place], ysend.at[j], yrecv.at[place],
                      (t, lax.rem(s + j, S)))

    @pl.when(works)
    def _():
        @pl.when(has_down)
        def _():
            for c in low_c:
                c.wait_recv()
            lax.fori_loop(0, H - 1, fill, 0)
            low0.wait_recv()

        @pl.when(has_up)
        def _():
            for c in high_c:
                c.wait_recv()
            lax.fori_loop(H - 1 + depth, 2 * H - 2 + depth, fill, 0)
            high0.wait_recv()

        @pl.when(s == 0)
        def _():
            lax.fori_loop(0, H - 1, fill, 0)

        @pl.when(s == S - 1)
        def _():
            lax.fori_loop(H - 1 + depth, 2 * H - 2 + depth, fill, 0)

        main0.wait_recv()

        for r, d in enumerate(ROUNDS):
            if r > 0:
                low = remote(U.at[r, pl.ds(H + depth - d, d)], U.at[r, pl.ds(H - d, d)],
                             hsend.at[r, 0], hrecv.at[r, 0], (t, up_s))
                high = remote(U.at[r, pl.ds(H, d)], U.at[r, pl.ds(H + depth, d)],
                              hsend.at[r, 1], hrecv.at[r, 1], (t, down_s))

                @pl.when(has_up)
                def _(low=low):
                    low.start()

                @pl.when(has_down)
                def _(high=high):
                    high.start()

                @pl.when(has_down)
                def _(low=low):
                    low.wait_recv()

                @pl.when(has_up)
                def _(high=high):
                    high.wait_recv()
            src = U.at[r]
            for j in range(1, d + 1):
                dst = U.at[r + 1] if j == d else V.at[j % 2]
                step(src, dst, H - d + j, H + depth + d - j)
                src = dst
            if r > 0:
                @pl.when(has_up)
                def _(low=low):
                    low.wait_send()

                @pl.when(has_down)
                def _(high=high):
                    high.wait_send()

        R = len(ROUNDS)
        sums = []
        for p in range(planes):
            total = None
            for z in range(B * p, B * p + B):
                f = U[R, H + z] - st[z]
                F[z] = f
                total = f if total is None else total + f
            sums.append(total)
        wloc[...] = pool(jnp.concatenate(sums, axis=0), pad_rows)
        pl.semaphore_wait(ready, S - 1)

        for j in range(T):
            for k in range(S):
                if j or k:
                    w_copy(j, k, t, s).start()
        wg[pl.ds(s, 1), pl.ds(t, 1)] = wloc[...][None, None]

        wide = prolong(wloc[...], planes * Y, 0)
        q = jnp.zeros((8, X), jnp.float32)
        for p in range(planes):
            mean = wide[p * Y : (p + 1) * Y]
            for z in range(B * p, B * p + B):
                g = F[z] - mean
                q += jnp.sum((g * g).reshape(Y // 8, 8, X), axis=0)
        qloc[...] = jnp.sum(q, axis=0, keepdims=True)

        for j in range(1, T):
            q_copy(j, t).start()
        qg[pl.ds(t, 1)] = qloc[...][None]

    @pl.when(t == 0)
    def _():
        pl.semaphore_wait(ready, S - 1)

    for j in range(1, S):
        cc_copy(j, lax.rem(s + S - j, S)).wait_recv()
    for p in range(S):
        cfull[:, p * slab_rows : (p + 1) * slab_rows] = ccg[p, :, 0:slab_rows]
    rows = S * slab_rows
    crow = iota((rows, X), 0)
    clane = iota((rows, X), 1)
    cols = X // B
    group = clane // cols
    y_high = lax.rem(crow, plane_rows)
    courant = FSTEPS / (4.0 * GC)
    spread = FSTEPS / (16.0 * GC)
    for i, w in enumerate(weights(
        cfull[0] * courant, cfull[1] * courant, cfull[2] * courant, cfull[3] * spread,
        (
            lax.rem(clane, cols) == 0,
            lax.rem(clane, cols) == cols - 1,
            (y_high == 0) & (group == 0),
            (y_high == plane_rows - 1) & (group == B - 1),
            crow < plane_rows,
            crow >= rows - plane_rows,
        ),
    )):
        cw[i] = w

    def coarse(u):
        for _ in range(GC):
            below = jnp.where(group == B - 1, pltpu.roll(u, 1, 0), u)
            above = jnp.where(group == 0, pltpu.roll(u, rows - 1, 0), u)
            v = cw[0] * u
            v += cw[1] * pltpu.roll(u, 1, 1)
            v += cw[2] * pltpu.roll(u, X - 1, 1)
            v += cw[3] * pltpu.roll(below, cols, 1)
            v += cw[4] * pltpu.roll(above, X - cols, 1)
            v += cw[5] * pltpu.roll(u, plane_rows, 0)
            v += cw[6] * pltpu.roll(u, rows - plane_rows, 0)
            u = v
        return u

    total = jnp.zeros((1, X), jnp.float32)
    for m in range(1, T):

        @pl.when(t != m)
        def _(m=m):
            q_copy(1, m).wait_recv()

        total = total + qg[m]
    qsum[...] = total
    for j in range(1, S):
        sum_copy(j, s).start()

    def chain(m, carry):
        jump, squares = carry
        for p in range(S):
            @pl.when((t != m) | (s != p))
            def _(p=p):
                w_copy(1, 0, m, p).wait_recv()

        for p in range(S):
            full[p * slab_rows : (p + 1) * slab_rows] = wg[p, m, 0:slab_rows]
        moved = coarse(jump)
        hs[m] = moved
        jump = full[...] + moved
        return jump, squares + jump * jump

    zero = jnp.zeros((rows, X), jnp.float32)
    _, squares = lax.fori_loop(1, T, chain, (zero, zero))

    @pl.when(works)
    def _():
        wide = prolong(hs[t], planes * Y, s * slab_rows)
        for z in range(depth):
            p = z // B
            out_ref[0, z] = U[len(ROUNDS), H + z] + wide[p * Y : (p + 1) * Y]

    @pl.when(t == 0)
    def _():
        out_ref[0] = st[...]

    for j in range(1, S):
        place = lax.rem(s + S - j, S)
        sum_copy(j, place).wait_recv()
        total = total + qsums[place]
    total = total + float(B**3) * jnp.sum(squares, axis=0, keepdims=True)
    total = jnp.sum(total, axis=1, keepdims=True)
    count = N * depth * Y * X
    chg_ref[...] = jnp.sqrt(total / count + 1e-6)

    for j in range(1, S):
        cc_copy(j, s).wait_send()
        sum_copy(j, s).wait_send()

    @pl.when(moves)
    def _():
        main0.wait_send()

    @pl.when(moves & has_up)
    def _():
        low0.wait_send()

    @pl.when(moves & has_down)
    def _():
        high0.wait_send()

    @pl.when(works & has_up)
    def _():
        for c in low_c:
            c.wait_send()

    @pl.when(works & has_down)
    def _():
        for c in high_c:
            c.wait_send()

    @pl.when(works)
    def _():
        for j in range(1, T):
            q_copy(j, t).wait_send()
        for j in range(T):
            for k in range(S):
                if j or k:
                    w_copy(j, k, t, s).wait_send()


def per_device(T, S, starts, vel_x, vel_y, vel_z, kappa):
    depth, Y, X = vel_x.shape
    slab_rows = depth // B * Y // B**2
    pad_rows = -(-slab_rows // 8) * 8
    rows = S * slab_rows
    R = len(ROUNDS)
    vmem = lambda *shape: pltpu.VMEM(shape, jnp.float32)
    dma = lambda *shape: pltpu.SemaphoreType.DMA(shape)
    ext = depth + 2 * HALO
    new, change = pl.pallas_call(
        functools.partial(kernel, T, S),
        out_shape=(
            jax.ShapeDtypeStruct(starts.shape, jnp.float32),
            jax.ShapeDtypeStruct((1, 1), jnp.float32),
        ),
        in_specs=[pl.BlockSpec(memory_space=pl.ANY)] * 5,
        out_specs=(
            pl.BlockSpec(memory_space=pltpu.VMEM),
            pl.BlockSpec(memory_space=pltpu.VMEM),
        ),
        scratch_shapes=[
            vmem(4, ext - 2, Y, X),
            vmem(7, ext - 2, Y, X),
            vmem(R + 1, ext, Y, X),
            vmem(2, ext, Y, X),
            vmem(depth, Y, X),
            vmem(depth, Y, X),
            vmem(pad_rows, X),
            vmem(S, T, pad_rows, X),
            vmem(4, pad_rows, X),
            vmem(S, 4, pad_rows, X),
            vmem(1, X),
            vmem(T, 1, X),
            vmem(1, X),
            vmem(S, 1, X),
            vmem(rows, X),
            vmem(4, rows, X),
            vmem(7, rows, X),
            vmem(T, rows, X),
            dma(5),
            dma(3), dma(3),
            dma(2, 4), dma(2, 4),
            dma(R, 2), dma(R, 2),
            dma(S), dma(S),
            dma(T, S), dma(S, T),
            dma(T), dma(T),
            dma(S), dma(S),
            pltpu.SemaphoreType.REGULAR,
        ],
        compiler_params=pltpu.CompilerParams(
            collective_id=0, has_side_effects=True, vmem_limit_bytes=60 * 2**20
        ),
    )(starts, vel_x, vel_y, vel_z, kappa)
    return new, change[0, 0]


def solution(mesh):
    T, S = mesh.shape["tm"], mesh.shape["space"]
    return jax.shard_map(
        functools.partial(per_device, T, S),
        mesh=mesh,
        in_specs=(
            P("tm", "space", None, None),
            P("space", None, None),
            P("space", None, None),
            P("space", None, None),
            P("space", None, None),
        ),
        out_specs=(P("tm", "space", None, None), P()),
        check_vma=False,
    )
```

```python
import functools

import jax
import jax.numpy as jnp
from jax import lax
from jax.experimental import pallas as pl
from jax.experimental.pallas import tpu as pltpu
from jax.sharding import PartitionSpec as P

FSTEPS = 6
GC = 2
B = 4
ROUNDS = (3, 3)
HALO = max(ROUNDS)
STEP_PLANES = (16, 14, 12, 7, 4, 2, 1)
MESH = pl.DeviceIdType.MESH


def dot(a, b):
    return jnp.dot(
        a, b, precision=lax.Precision.HIGHEST, preferred_element_type=jnp.float32
    )


def iota(shape, dim):
    return lax.broadcasted_iota(jnp.int32, shape, dim)


def group_mask(rows, lanes):
    group = (iota((rows, lanes), 0) // B) % B
    return group == iota((rows, lanes), 1) // (lanes // B)


def pool(sums, packed_rows):
    rows, lanes = sums.shape
    cols = lanes // B
    spread = iota((lanes, lanes), 0) // B == iota((lanes, lanes), 1) % cols
    wide = dot(sums, jnp.where(spread, 1.0 / B**3, 0.0).astype(jnp.float32))
    wide = jnp.where(group_mask(rows, lanes), wide, 0.0)
    pick = iota((packed_rows, rows), 1) // B**2 == iota((packed_rows, rows), 0)
    return dot(pick.astype(jnp.float32), wide)


def prolong(packed, rows, first):
    lanes = packed.shape[1]
    cols = lanes // B
    shape = (rows, packed.shape[0])
    pick = iota(shape, 0) // B**2 + first == iota(shape, 1)
    wide = dot(pick.astype(jnp.float32), packed)
    wide = jnp.where(group_mask(rows, lanes), wide, 0.0)
    spread = iota((lanes, lanes), 0) % cols == iota((lanes, lanes), 1) // B
    return dot(wide, spread.astype(jnp.float32))


def weights(vx, vy, vz, k, edges):
    low_x, high_x, low_y, high_y, low_z, high_z = edges

    def inside(edge, value):
        return value if edge is None else jnp.where(edge, 0.0, value)

    return (
        1.0 - jnp.abs(vx) - jnp.abs(vy) - jnp.abs(vz) - 6.0 * k,
        inside(low_x, k + jnp.maximum(vx, 0.0)),
        inside(high_x, k - jnp.minimum(vx, 0.0)),
        inside(low_y, k + jnp.maximum(vy, 0.0)),
        inside(high_y, k - jnp.minimum(vy, 0.0)),
        inside(low_z, k + jnp.maximum(vz, 0.0)),
        inside(high_z, k - jnp.minimum(vz, 0.0)),
    )


def kernel(
    T, S,
    st_hbm, vx_hbm, vy_hbm, vz_hbm, kp_hbm,
    out_ref, chg_ref,
    cx, co, U, V, st, F, wloc, wg, ccloc, ccg, qloc, qg, qsum, qsums, full, cfull, cw, hs,
    lsem, usend, urecv, csend, crecv, hsend, hrecv, ccsend, ccrecv,
    wsend, wrecv, qsend, qrecv, ysend, yrecv, ready, fsend, frecv,
):
    depth, Y, X = st.shape
    N = T * S
    t = lax.axis_index("tm")
    s = lax.axis_index("space")
    planes = depth // B
    slab_rows = planes * Y // B**2
    plane_rows = Y // B**2
    pad_rows = wloc.shape[0]
    H = HALO
    coefs = (vx_hbm, vy_hbm, vz_hbm, kp_hbm)

    loads = [
        pltpu.make_async_copy(c, cx.at[i, pl.ds(H - 1, depth)], lsem.at[i])
        for i, c in enumerate(coefs)
    ]
    load_st = pltpu.make_async_copy(st_hbm.at[0], st, lsem.at[4])
    for c in loads:
        c.start()
    load_st.start()

    barrier = pltpu.get_barrier_semaphore()

    up_t = lax.rem(t + 1, T)
    down_t = lax.rem(t + T - 1, T)
    up_s = lax.rem(s + 1, S)
    down_s = lax.rem(s + S - 1, S)
    has_up = s < S - 1
    has_down = s > 0
    moves = t < T - 1
    works = t > 0

    def greet(device):
        pl.semaphore_signal(barrier, inc=1, device_id=device, device_id_type=MESH)

    @pl.when(works & has_up)
    def _():
        greet((down_t, up_s))

    @pl.when(works & has_down)
    def _():
        greet((down_t, down_s))

    for j in range(1, T):
        greet((lax.rem(t + j, T), s))
    for j in range(1, S):
        greet((t, lax.rem(s + j, S)))

    @pl.when(s == 0)
    def _():
        for r in range(len(ROUNDS)):
            U[r, 0:H] = jnp.zeros((H, Y, X), jnp.float32)
        if H > 1:
            cx[:, 0 : H - 1] = jnp.zeros((4, H - 1, Y, X), jnp.float32)

    @pl.when(s == S - 1)
    def _():
        for r in range(len(ROUNDS)):
            U[r, H + depth : 2 * H + depth] = jnp.zeros((H, Y, X), jnp.float32)
        if H > 1:
            cx[:, H - 1 + depth : 2 * H - 2 + depth] = jnp.zeros((4, H - 1, Y, X), jnp.float32)

    for c in loads:
        c.wait()
    load_st.wait()

    lane = iota((Y, X), 1)
    row = iota((Y, X), 0)
    edges = (lane == 0, lane == X - 1, row == 0, row == Y - 1, None, None)

    def fill(z, _):
        for i, w in enumerate(weights(cx[0, z], cx[1, z], cx[2, z], cx[3, z], edges)):
            co[i, z] = w
        return 0

    lax.fori_loop(H - 1, H - 1 + depth, fill, 0)

    for i in range(4):
        sums = [
            cx[i, H - 1 + B * p] + cx[i, H + B * p] + cx[i, H + 1 + B * p] + cx[i, H + 2 + B * p]
            for p in range(planes)
        ]
        ccloc[i] = pool(jnp.concatenate(sums, axis=0), pad_rows)
    ccg[pl.ds(s, 1)] = ccloc[...][None]

    across = jnp.where(has_up, 1, 0) + jnp.where(has_down, 1, 0)
    pl.semaphore_wait(barrier, T + S - 2 + jnp.where(moves, across, 0))

    for j in range(1, S):
        pl.semaphore_signal(
            ready, inc=1, device_id=(t, lax.rem(s + j, S)), device_id_type=MESH
        )

    def remote(src, dst, send, recv, device):
        return pltpu.make_async_remote_copy(
            src_ref=src, dst_ref=dst, send_sem=send, recv_sem=recv,
            device_id=device, device_id_type=MESH,
        )

    d0 = ROUNDS[0]
    low0 = remote(st_hbm.at[0, pl.ds(depth - d0, d0)], U.at[0, pl.ds(H - d0, d0)],
                  usend.at[0], urecv.at[0], (up_t, up_s))
    high0 = remote(st_hbm.at[0, pl.ds(0, d0)], U.at[0, pl.ds(H + depth, d0)],
                   usend.at[1], urecv.at[1], (up_t, down_s))
    main0 = remote(st_hbm.at[0], U.at[0, pl.ds(H, depth)],
                   usend.at[2], urecv.at[2], (up_t, s))
    low_c = [
        remote(c.at[pl.ds(depth - H + 1, H - 1)], cx.at[i, pl.ds(0, H - 1)],
               csend.at[0, i], crecv.at[0, i], (t, up_s))
        for i, c in enumerate(coefs)
    ] if H > 1 else []
    high_c = [
        remote(c.at[pl.ds(0, H - 1)], cx.at[i, pl.ds(H - 1 + depth, H - 1)],
               csend.at[1, i], crecv.at[1, i], (t, down_s))
        for i, c in enumerate(coefs)
    ] if H > 1 else []

    half = lax.rem(t, 2)
    pair = t + 1 - 2 * half
    low_f = [
        remote(cx.at[i, pl.ds(0, H - 1)], cx.at[i, pl.ds(0, H - 1)],
               fsend.at[0, i], frecv.at[0, i], (pair, s))
        for i in range(4)
    ]
    high_f = [
        remote(cx.at[i, pl.ds(H - 1 + depth, H - 1)], cx.at[i, pl.ds(H - 1 + depth, H - 1)],
               fsend.at[1, i], frecv.at[1, i], (pair, s))
        for i in range(4)
    ]

    def for_mine(cond, *acts):
        for h in range(2):
            @pl.when((half == h) & cond)
            def _(h=h):
                for i in (2 * h, 2 * h + 1):
                    for act in acts:
                        act(i)

    def for_others(cond, act):
        for h in range(2):
            @pl.when((half != h) & cond)
            def _(h=h):
                for i in (2 * h, 2 * h + 1):
                    act(i)

    for_mine(has_up, lambda i: low_c[i].start())
    for_mine(has_down, lambda i: high_c[i].start())

    @pl.when(moves & has_up)
    def _():
        low0.start()

    @pl.when(moves & has_down)
    def _():
        high0.start()

    @pl.when(moves)
    def _():
        main0.start()

    def cc_copy(j, slot):
        return remote(ccloc, ccg.at[slot], ccsend.at[j], ccrecv.at[slot],
                      (t, lax.rem(s + j, S)))

    for j in range(1, S):
        cc_copy(j, s).start()

    def step(src, dst, lo, hi):
        group = next(g for g in STEP_PLANES if (hi - lo) % g == 0)

        def body(i, _):
            z = lo + i * group
            u = [src[z - 1 + k] for k in range(group + 2)]
            new = []
            for k in range(group):
                c, n = u[k + 1], z - 1 + k
                v = co[0, n] * c + co[5, n] * u[k] + co[6, n] * u[k + 2]
                v += co[3, n] * pltpu.roll(c, 1, 0) + co[4, n] * pltpu.roll(c, Y - 1, 0)
                v += co[1, n] * pltpu.roll(c, 1, 1) + co[2, n] * pltpu.roll(c, X - 1, 1)
                new.append(v)
            for k in range(group):
                dst[z + k] = new[k]
            return 0

        lax.fori_loop(0, (hi - lo) // group, body, 0)

    def w_copy(j, k, slice_from, place):
        return remote(wloc.at[pl.ds(0, slab_rows)],
                      wg.at[place, slice_from, pl.ds(0, slab_rows)],
                      wsend.at[j, k], wrecv.at[place, slice_from],
                      (lax.rem(t + j, T), lax.rem(s + k, S)))

    def q_copy(j, slice_from):
        return remote(qloc, qg.at[slice_from], qsend.at[j], qrecv.at[slice_from],
                      (lax.rem(t + j, T), s))

    def sum_copy(j, place):
        return remote(qsum, qsums.at[place], ysend.at[j], yrecv.at[place],
                      (t, lax.rem(s + j, S)))

    for_mine(has_down, lambda i: low_c[i].wait_recv(), lambda i: low_f[i].start())
    for_mine(has_up, lambda i: high_c[i].wait_recv(), lambda i: high_f[i].start())
    for_others(has_down, lambda i: low_f[i].wait_recv())
    for_others(has_up, lambda i: high_f[i].wait_recv())

    @pl.when(works)
    def _():
        lax.fori_loop(0, H - 1, fill, 0)
        lax.fori_loop(H - 1 + depth, 2 * H - 2 + depth, fill, 0)

        @pl.when(has_down)
        def _():
            low0.wait_recv()

        @pl.when(has_up)
        def _():
            high0.wait_recv()

        main0.wait_recv()

        for r, d in enumerate(ROUNDS):
            if r > 0:
                low = remote(U.at[r, pl.ds(H + depth - d, d)], U.at[r, pl.ds(H - d, d)],
                             hsend.at[r, 0], hrecv.at[r, 0], (t, up_s))
                high = remote(U.at[r, pl.ds(H, d)], U.at[r, pl.ds(H + depth, d)],
                              hsend.at[r, 1], hrecv.at[r, 1], (t, down_s))

                @pl.when(has_up)
                def _(low=low):
                    low.start()

                @pl.when(has_down)
                def _(high=high):
                    high.start()

                @pl.when(has_down)
                def _(low=low):
                    low.wait_recv()

                @pl.when(has_up)
                def _(high=high):
                    high.wait_recv()
            src = U.at[r]
            for j in range(1, d + 1):
                dst = U.at[r + 1] if j == d else V.at[j % 2]
                step(src, dst, H - d + j, H + depth + d - j)
                src = dst
            if r > 0:
                @pl.when(has_up)
                def _(low=low):
                    low.wait_send()

                @pl.when(has_down)
                def _(high=high):
                    high.wait_send()

        R = len(ROUNDS)
        sums = []
        for p in range(planes):
            total = None
            for z in range(B * p, B * p + B):
                f = U[R, H + z] - st[z]
                F[z] = f
                total = f if total is None else total + f
            sums.append(total)
        wloc[...] = pool(jnp.concatenate(sums, axis=0), pad_rows)
        pl.semaphore_wait(ready, S - 1)

        for j in range(T):
            for k in range(S):
                if j or k:
                    w_copy(j, k, t, s).start()
        wg[pl.ds(s, 1), pl.ds(t, 1)] = wloc[...][None, None]

        wide = prolong(wloc[...], planes * Y, 0)
        q = jnp.zeros((8, X), jnp.float32)
        for p in range(planes):
            mean = wide[p * Y : (p + 1) * Y]
            for z in range(B * p, B * p + B):
                g = F[z] - mean
                q += jnp.sum((g * g).reshape(Y // 8, 8, X), axis=0)
        qloc[...] = jnp.sum(q, axis=0, keepdims=True)

        for j in range(1, T):
            q_copy(j, t).start()
        qg[pl.ds(t, 1)] = qloc[...][None]

    @pl.when(t == 0)
    def _():
        pl.semaphore_wait(ready, S - 1)

    for j in range(1, S):
        cc_copy(j, lax.rem(s + S - j, S)).wait_recv()
    for p in range(S):
        cfull[:, p * slab_rows : (p + 1) * slab_rows] = ccg[p, :, 0:slab_rows]
    rows = S * slab_rows
    crow = iota((rows, X), 0)
    clane = iota((rows, X), 1)
    cols = X // B
    group = clane // cols
    y_high = lax.rem(crow, plane_rows)
    courant = FSTEPS / (4.0 * GC)
    spread = FSTEPS / (16.0 * GC)
    for i, w in enumerate(weights(
        cfull[0] * courant, cfull[1] * courant, cfull[2] * courant, cfull[3] * spread,
        (
            lax.rem(clane, cols) == 0,
            lax.rem(clane, cols) == cols - 1,
            (y_high == 0) & (group == 0),
            (y_high == plane_rows - 1) & (group == B - 1),
            crow < plane_rows,
            crow >= rows - plane_rows,
        ),
    )):
        cw[i] = w

    def coarse(u):
        for _ in range(GC):
            below = jnp.where(group == B - 1, pltpu.roll(u, 1, 0), u)
            above = jnp.where(group == 0, pltpu.roll(u, rows - 1, 0), u)
            v = cw[0] * u
            v += cw[1] * pltpu.roll(u, 1, 1)
            v += cw[2] * pltpu.roll(u, X - 1, 1)
            v += cw[3] * pltpu.roll(below, cols, 1)
            v += cw[4] * pltpu.roll(above, X - cols, 1)
            v += cw[5] * pltpu.roll(u, plane_rows, 0)
            v += cw[6] * pltpu.roll(u, rows - plane_rows, 0)
            u = v
        return u

    total = jnp.zeros((1, X), jnp.float32)
    for m in range(1, T):

        @pl.when(t != m)
        def _(m=m):
            q_copy(1, m).wait_recv()

        total = total + qg[m]
    qsum[...] = total
    for j in range(1, S):
        sum_copy(j, s).start()

    def chain(m, carry):
        jump, squares = carry
        for p in range(S):
            @pl.when((t != m) | (s != p))
            def _(p=p):
                w_copy(1, 0, m, p).wait_recv()

        for p in range(S):
            full[p * slab_rows : (p + 1) * slab_rows] = wg[p, m, 0:slab_rows]
        moved = coarse(jump)
        hs[m] = moved
        jump = full[...] + moved
        return jump, squares + jump * jump

    zero = jnp.zeros((rows, X), jnp.float32)
    _, squares = lax.fori_loop(1, T, chain, (zero, zero))

    @pl.when(works)
    def _():
        wide = prolong(hs[t], planes * Y, s * slab_rows)
        for z in range(depth):
            p = z // B
            out_ref[0, z] = U[len(ROUNDS), H + z] + wide[p * Y : (p + 1) * Y]

    @pl.when(t == 0)
    def _():
        out_ref[0] = st[...]

    for j in range(1, S):
        place = lax.rem(s + S - j, S)
        sum_copy(j, place).wait_recv()
        total = total + qsums[place]
    total = total + float(B**3) * jnp.sum(squares, axis=0, keepdims=True)
    total = jnp.sum(total, axis=1, keepdims=True)
    count = N * depth * Y * X
    chg_ref[...] = jnp.sqrt(total / count + 1e-6)

    for j in range(1, S):
        cc_copy(j, s).wait_send()
        sum_copy(j, s).wait_send()

    @pl.when(moves)
    def _():
        main0.wait_send()

    @pl.when(moves & has_up)
    def _():
        low0.wait_send()

    @pl.when(moves & has_down)
    def _():
        high0.wait_send()

    for_mine(has_up, lambda i: low_c[i].wait_send(), lambda i: high_f[i].wait_send())
    for_mine(has_down, lambda i: high_c[i].wait_send(), lambda i: low_f[i].wait_send())

    @pl.when(works)
    def _():
        for j in range(1, T):
            q_copy(j, t).wait_send()
        for j in range(T):
            for k in range(S):
                if j or k:
                    w_copy(j, k, t, s).wait_send()


def per_device(T, S, starts, vel_x, vel_y, vel_z, kappa):
    depth, Y, X = vel_x.shape
    slab_rows = depth // B * Y // B**2
    pad_rows = -(-slab_rows // 8) * 8
    rows = S * slab_rows
    R = len(ROUNDS)
    vmem = lambda *shape: pltpu.VMEM(shape, jnp.float32)
    dma = lambda *shape: pltpu.SemaphoreType.DMA(shape)
    ext = depth + 2 * HALO
    new, change = pl.pallas_call(
        functools.partial(kernel, T, S),
        out_shape=(
            jax.ShapeDtypeStruct(starts.shape, jnp.float32),
            jax.ShapeDtypeStruct((1, 1), jnp.float32),
        ),
        in_specs=[pl.BlockSpec(memory_space=pl.ANY)] * 5,
        out_specs=(
            pl.BlockSpec(memory_space=pltpu.VMEM),
            pl.BlockSpec(memory_space=pltpu.VMEM),
        ),
        scratch_shapes=[
            vmem(4, ext - 2, Y, X),
            vmem(7, ext - 2, Y, X),
            vmem(R + 1, ext, Y, X),
            vmem(2, ext, Y, X),
            vmem(depth, Y, X),
            vmem(depth, Y, X),
            vmem(pad_rows, X),
            vmem(S, T, pad_rows, X),
            vmem(4, pad_rows, X),
            vmem(S, 4, pad_rows, X),
            vmem(1, X),
            vmem(T, 1, X),
            vmem(1, X),
            vmem(S, 1, X),
            vmem(rows, X),
            vmem(4, rows, X),
            vmem(7, rows, X),
            vmem(T, rows, X),
            dma(5),
            dma(3), dma(3),
            dma(2, 4), dma(2, 4),
            dma(R, 2), dma(R, 2),
            dma(S), dma(S),
            dma(T, S), dma(S, T),
            dma(T), dma(T),
            dma(S), dma(S),
            pltpu.SemaphoreType.REGULAR,
            dma(2, 4), dma(2, 4),
        ],
        compiler_params=pltpu.CompilerParams(
            collective_id=0, has_side_effects=True, vmem_limit_bytes=60 * 2**20
        ),
    )(starts, vel_x, vel_y, vel_z, kappa)
    return new, change[0, 0]


def solution(mesh):
    T, S = mesh.shape["tm"], mesh.shape["space"]
    return jax.shard_map(
        functools.partial(per_device, T, S),
        mesh=mesh,
        in_specs=(
            P("tm", "space", None, None),
            P("space", None, None),
            P("space", None, None),
            P("space", None, None),
            P("space", None, None),
        ),
        out_specs=(P("tm", "space", None, None), P()),
        check_vma=False,
    )
```
